128 devices in a mesh: inner: 8 (over y_lo, x), outer: 16 (over y_hi, z, core).
Axes of the slice: x: 4, y: 4 (y_hi: 2, y_lo: 2; y = y_hi * 2 + y_lo), z: 4, core: 2. Of those that a mesh axis runs over, the one named last changes fastest.
Arguments:
- queries: bfloat16 [16384, 8192], P(('inner', 'outer')), may hold values from -6 to 6
- keys: bfloat16 [16384, 1024], P(('inner', 'outer')), may hold values from -6 to 6
- values: bfloat16 [16384, 1024], P(('inner', 'outer')), may hold values from -6 to 6
- grad_out: bfloat16 [16384, 8192], P(('inner', 'outer')), may hold values from -6 to 6
- doc_ids: int32 [16384], replicated, may hold values from 0 to 31, never falling along the last dimension, each value on 1 to 1024 neighbouring positions
Outputs:
- grad_queries: bfloat16 [16384, 8192], P(('inner', 'outer'))
- grad_keys: bfloat16 [16384, 1024], P(('inner', 'outer'))
- grad_values: bfloat16 [16384, 1024], P(('inner', 'outer'))
The draws below stay inside these ranges and needn't reach their ends.
Inputs may be any that keep to these rules, and one draw needn't show every extreme that they name: `doc_ids`: document numbers never fall along the sequence; each document has 1 to 1024 tokens and one has exactly 1024.
All inputs are finite; a program needn't handle non-finite values.
Results may differ from the reference program's by a relative error of at most 0.011.
The reference program's roundings to bfloat16 on the way (of `probs_b`, `attn_out` and `dscores`) count: a program that leaves them out, or rounds other values in their place, can miss the bound.
Values may be sent and summed in bfloat16 or wider, within the bound.
No kernel may reach another device: no remote copies, remote signals or barrier semaphores. Data moves between devices by JAX's collectives and lax.ppermute only.
A program may use at most 64 MiB of HBM per device.

```python
import math
import jax
import jax.numpy as jnp
import numpy as np
from jax import lax

H = 64
KVH = 8
HD = 128
TOK_DEV = 128
G = 8
TOKENS = 16384
WINDOW = 384
DOCS = 32
DOC_MOST = 1024


def draw_queries(key, part):
    key = jax.random.fold_in(key, 11)
    base = jnp.clip(jax.random.normal(key, (TOKENS, H, HD), jnp.float32), -6.0, 6.0)
    return base.reshape(TOKENS, H * HD).astype(jnp.bfloat16)


def draw_keys(key, part):
    key = jax.random.fold_in(key, 23)
    base = jnp.clip(jax.random.normal(key, (TOKENS, KVH, HD), jnp.float32), -6.0, 6.0)
    return base.reshape(TOKENS, KVH * HD).astype(jnp.bfloat16)


def steps_of(stream_key, shape, shards, least, top_value):
    def one(axis_at, blocks):
        heights = jax.random.uniform(jax.random.fold_in(jax.random.fold_in(stream_key, 6), axis_at), (blocks,), jnp.float32, least / len(shards), top_value / len(shards))
        return jnp.repeat(jnp.exp(heights), shape[axis_at] // blocks).reshape((-1,) + (1,) * (len(shape) - axis_at - 1))

    level = one(*shards[0])
    for cut in shards[1:]:
        level = level * one(*cut)
    return level


def length_profile(amount, total, limit, slope):
    portions = [(1 << 20) // math.isqrt(rank ** slope) + 1 for rank in range(2, amount + 1)]
    rest, given = total - limit - (amount - 1), [1] * (amount - 1)
    while rest > 0:
        candidates = [i for i in range(amount - 1) if given[i] < limit]
        pool, budget = sum([portions[i] for i in candidates]), rest
        for i in candidates:
            extra = min(limit - given[i], max(1, budget * portions[i] // pool), rest)
            given[i] = given[i] + extra
            rest = rest - extra
    return np.array([limit] + given)


def ragged_sizes(stream_key, number_of, total, bound, slope):
    if number_of == 2:
        one = jax.random.randint(stream_key, (), max(1, total - bound), min(bound, total - 1) + 1)
        return jnp.stack([one, total - one])
    tallies = jnp.asarray(length_profile(number_of, total, bound, slope), jnp.int32)
    pairs = (number_of - 1) // 2
    source_of, sink = tallies[1:1 + 2 * pairs:2], tallies[2:2 + 2 * pairs:2]
    room = jnp.minimum(source_of - 1, bound - sink)
    passed = jax.random.randint(jax.random.fold_in(stream_key, 1), (pairs,), 0, 1 << 20) % (room + 1)
    tallies = tallies.at[1:1 + 2 * pairs:2].set(source_of - passed).at[2:2 + 2 * pairs:2].set(sink + passed)
    return tallies[jax.random.permutation(jax.random.fold_in(stream_key, 2), number_of)]


def centred(key, shape, scale, limit, pieces=(), kind=jnp.bfloat16):
    drawn = jax.random.normal(key, shape, jnp.float32) * scale
    if len(pieces) > 0:
        drawn = steps_of(key, shape, pieces, -0.22, 0.18) * drawn
    return jnp.clip(drawn, min=-limit, max=limit).astype(kind)


def setup_inputs(seed: int = 0) -> dict:
    splits = jax.random.split(jax.random.key(seed), 6)
    return {
        "queries": draw_queries(jax.random.fold_in(splits[5], 71), 0),
        "keys": draw_keys(jax.random.fold_in(splits[5], 71), 0),
        "values": centred(splits[2], (TOKENS, KVH * HD), 1.0, 6.0, ((0, 128),)),
        "grad_out": centred(splits[3], (TOKENS, H * HD), 1.0, 6.0, ((0, 128),)),
        "doc_ids": jnp.searchsorted(jnp.cumsum(ragged_sizes(splits[4], DOCS, TOKENS, DOC_MOST, 2)), jnp.arange(TOKENS), side="right").astype(jnp.int32),
    }


def product(form, left, right):
    return jnp.einsum(form, left.astype(jnp.float32), right.astype(jnp.float32))


def block_grads(query_rows, dout_rows, key_rows, value_rows, query_pos, key_pos, query_doc, key_doc):
    count = query_rows.shape[0]
    span = key_rows.shape[0]
    scale = 1.0 / (HD ** 0.5)
    gap = query_pos[:, None] - key_pos[None, :]
    visible = (gap >= 0) & (gap < WINDOW) & (key_pos[None, :] >= 0) & (query_doc[:, None] == key_doc[None, :])
    dq_parts = []
    dk_parts = []
    dv_parts = []
    for group in range(KVH):
        qh = query_rows[:, group * G * HD:(group + 1) * G * HD].reshape(count, G, HD)
        dh = dout_rows[:, group * G * HD:(group + 1) * G * HD].reshape(count, G, HD)
        kh = key_rows[:, group * HD:(group + 1) * HD]
        vh = value_rows[:, group * HD:(group + 1) * HD]
        scores = product("rgd,kd->grk", qh, kh) * scale
        masked = jnp.where(visible[None], scores, -jnp.inf)
        top = jnp.max(masked, axis=-1, keepdims=True)
        total = jnp.sum(jnp.where(visible[None], jnp.exp(scores - top), 0.0), axis=-1, keepdims=True)
        lse = top + jnp.log(total)
        probs = jnp.where(visible[None], jnp.exp(scores - lse), 0.0)
        probs_b = probs.astype(jnp.bfloat16)
        attn_out = product("grk,kd->rgd", probs_b, vh).astype(jnp.bfloat16)
        attn_out = lax.optimization_barrier(attn_out)
        delta = jnp.sum(dh.astype(jnp.float32) * attn_out.astype(jnp.float32), axis=-1)
        dprobs = product("rgd,kd->grk", dh, vh)
        dscores = (probs * (dprobs - jnp.transpose(delta)[:, :, None])).astype(jnp.bfloat16)
        dq_parts.append((product("grk,kd->rgd", dscores, kh) * scale).reshape(count, G * HD))
        dk_parts.append(product("grk,rgd->kd", dscores, qh) * scale)
        dv_parts.append(product("grk,rgd->kd", probs_b, dh))
    return (jnp.concatenate(dq_parts, axis=1).astype(jnp.bfloat16),
            jnp.concatenate(dk_parts, axis=1), jnp.concatenate(dv_parts, axis=1))


def reference(queries, keys, values, grad_out, doc_ids):
    rows = TOK_DEV
    blocks = TOKENS // rows
    margin = 3 * rows
    width = KVH * HD
    key_pad = jnp.concatenate([jnp.zeros((margin, width), jnp.bfloat16), keys], axis=0)
    value_pad = jnp.concatenate([jnp.zeros((margin, width), jnp.bfloat16), values], axis=0)
    doc_pad = jnp.concatenate([jnp.full((margin,), -1, jnp.int32), doc_ids.astype(jnp.int32)], axis=0)

    def visit(carry, block):
        dk_acc, dv_acc = carry
        start = (block * rows).astype(jnp.int32)
        query_rows = lax.dynamic_slice_in_dim(queries, start, rows, 0)
        dout_rows = lax.dynamic_slice_in_dim(grad_out, start, rows, 0)
        key_rows = lax.dynamic_slice_in_dim(key_pad, start, 4 * rows, 0)
        value_rows = lax.dynamic_slice_in_dim(value_pad, start, 4 * rows, 0)
        query_pos = start + jnp.arange(rows, dtype=jnp.int32)
        key_pos = start - margin + jnp.arange(4 * rows, dtype=jnp.int32)
        query_doc = lax.dynamic_slice_in_dim(doc_ids.astype(jnp.int32), start, rows, 0)
        key_doc = lax.dynamic_slice_in_dim(doc_pad, start, 4 * rows, 0)
        dq_rows, dk_part, dv_part = block_grads(query_rows, dout_rows, key_rows, value_rows,
                                                query_pos, key_pos, query_doc, key_doc)
        dk_acc = lax.dynamic_update_slice_in_dim(
            dk_acc, lax.dynamic_slice_in_dim(dk_acc, start, 4 * rows, 0) + dk_part, start, 0)
        dv_acc = lax.dynamic_update_slice_in_dim(
            dv_acc, lax.dynamic_slice_in_dim(dv_acc, start, 4 * rows, 0) + dv_part, start, 0)
        return (dk_acc, dv_acc), dq_rows

    start_acc = jnp.zeros((TOKENS + margin, width), jnp.float32)
    (dk_acc, dv_acc), dq_all = lax.scan(visit, (start_acc, start_acc), jnp.arange(blocks, dtype=jnp.int32))
    grad_queries = dq_all.reshape(TOKENS, H * HD)
    return grad_queries, dk_acc[margin:].astype(jnp.bfloat16), dv_acc[margin:].astype(jnp.bfloat16)
```

```python
import jax
import jax.numpy as jnp
from jax import lax
from jax.experimental import pallas as pl
from jax.experimental.pallas import tpu as pltpu
from jax.sharding import PartitionSpec as P

KVH = 8
HD = 128
G = 8
WINDOW = 384
ROWS = 128
SPAN = 4 * ROWS
STACK = G * ROWS
AXES = ("inner", "outer")
SCALE = 1.0 / HD**0.5
SCALE_LOG2 = 1.4426950408889634 / HD**0.5
HIDDEN = -1e30
NT = (((1,), (1,)), ((), ()))
GROUPS = 2
MIB = 2**20
VMEM = pl.BlockSpec(memory_space=pltpu.VMEM)


def head_columns(group):
    return pl.ds(pl.multiple_of(group * HD, HD), HD)


def stacked_blocks(refs, group):
    return jnp.concatenate([ref[:, head_columns(group)] for ref in refs], axis=0)


def heads_of(ref, group):
    return [ref[:, head_columns(group * G + h)] for h in range(G)]


def put_blocks(refs, group, value):
    for i, ref in enumerate(refs):
        ref[:, head_columns(group)] = value[i * ROWS : (i + 1) * ROWS].astype(ref.dtype)


def over_groups(step):
    def body(i, carry):
        step([i * GROUPS + j for j in range(GROUPS)])
        return carry

    lax.fori_loop(0, KVH // GROUPS, body, 0)


def put_bias(index, docs_ref, bias_ref):
    odd = lax.rem(index, 2)
    line = lax.broadcasted_iota(jnp.int32, (ROWS, ROWS), 0)
    lane = lax.broadcasted_iota(jnp.int32, (ROWS, ROWS), 1)

    def docs_of(block):
        row = docs_ref[pl.ds(jnp.maximum(block, 0), 1), :].astype(jnp.float32)
        return jnp.broadcast_to(row, (ROWS, ROWS))

    query_doc = docs_of(index)
    for i, offset in enumerate([3 - 2 * odd, 2, 1 + 2 * odd, 0]):
        gap = offset * ROWS + lane - line
        same = docs_of(index - offset).T == query_doc
        visible = (gap >= 0) & (gap < WINDOW) & (index >= offset) & same
        bias_ref[i * ROWS : (i + 1) * ROWS] = jnp.where(visible, 0.0, HIDDEN).astype(jnp.bfloat16)


def probs_kernel(index_ref, docs_ref, query_hbm, dout_hbm, *refs):
    key_refs, probs_ref, query_ref, dot_ref = refs[:4], refs[4], refs[5], refs[6]
    dv_refs, dout_ref, own_ref, bias_ref, sems, own_sem = refs[7:11], *refs[11:16]
    own_load = pltpu.make_async_copy(key_refs[3], own_ref, own_sem)
    own_load.start()
    key_refs = [*key_refs[:3], own_ref]
    row = lax.broadcasted_iota(jnp.int32, (ROWS, STACK), 0)
    column = lax.broadcasted_iota(jnp.int32, (ROWS, STACK), 1)
    identity = jnp.where((column & (ROWS - 1)) == row, 1.0, 0.0).astype(jnp.bfloat16)
    width = GROUPS * STACK

    def loads(i):
        part = pl.ds(pl.multiple_of(i * width, width), width)
        return (
            pltpu.make_async_copy(query_hbm.at[:, part], query_ref.at[:, part], sems.at[0, i]),
            pltpu.make_async_copy(dout_hbm.at[:, part], dout_ref.at[:, part], sems.at[1, i]),
        )

    for i in range(KVH // GROUPS):
        for copy in loads(i):
            copy.start()
    put_bias(index_ref[0], docs_ref, bias_ref)
    bias = bias_ref[...]
    own_load.wait()

    def step(i, carry):
        for copy in loads(i):
            copy.wait()
        groups = [i * GROUPS + j for j in range(GROUPS)]
        scores = []
        for g in groups:
            query_t = jnp.concatenate([head.T for head in heads_of(query_ref, g)], axis=1)
            scores.append(
                jnp.dot(
                    jnp.concatenate([stacked_blocks(key_refs, g), bias], axis=1),
                    jnp.concatenate([query_t, identity], axis=0),
                    preferred_element_type=jnp.float32,
                )
            )
        for g, score in zip(groups, scores):
            powers = jnp.exp2((score - jnp.max(score, axis=0, keepdims=True)) * SCALE_LOG2)
            probs = powers * (1.0 / jnp.sum(powers, axis=0, keepdims=True))
            probs_b = probs.astype(jnp.bfloat16)
            probs_ref[g] = probs_b
            heads = heads_of(dout_ref, g)
            dot_ref[g] = jnp.concatenate([head.T for head in heads], axis=1)
            dout = jnp.concatenate(heads, axis=0)
            put_blocks(dv_refs, g, jnp.dot(probs_b, dout, preferred_element_type=jnp.float32))
        return carry

    lax.fori_loop(0, KVH // GROUPS, step, 0)


def scores_kernel(query_ref, dot_ref, probs_ref, mark_ref, dv_aside_ref, *refs):
    value_refs, dscores_ref, near_ref, dk_refs = refs[:4], refs[4], refs[5], refs[6:9]
    near_ref[:, KVH * HD :] = dv_aside_ref[...]

    def step(groups):
        deltas, dprobs = [], []
        for g in groups:
            values = stacked_blocks(value_refs, g)
            out = jnp.dot(values.T, probs_ref[g], preferred_element_type=jnp.float32)
            out = out.astype(jnp.bfloat16).astype(jnp.float32)
            deltas.append(jnp.sum(out * dot_ref[g].astype(jnp.float32), axis=0, keepdims=True))
            dprobs.append(jnp.dot(values, dot_ref[g], preferred_element_type=jnp.float32))
        for g, delta, dprob in zip(groups, deltas, dprobs):
            dscores = (probs_ref[g].astype(jnp.float32) * (dprob - delta)).astype(jnp.bfloat16)
            dscores_ref[g] = dscores
            query = jnp.concatenate(heads_of(query_ref, g), axis=0)
            dk = jnp.dot(dscores, query, preferred_element_type=jnp.float32)
            put_blocks([near_ref, *dk_refs], g, dk * SCALE)

    over_groups(step)


def queries_kernel(dscores_ref, *refs):
    key_refs, dq_ref = refs[:4], refs[4]
    for g in range(GROUPS):
        keys = jnp.concatenate([ref[:, g * HD : (g + 1) * HD] for ref in key_refs], axis=0)
        dq = jnp.dot(keys.T, dscores_ref[g], preferred_element_type=jnp.float32) * SCALE
        for h in range(G):
            column = (g * G + h) * HD
            dq_ref[:, column : column + HD] = dq[:, h * HD : (h + 1) * HD].T.astype(dq_ref.dtype)


PAIRS = KVH * G * SPAN * ROWS


def cost(products, exponentials=0):
    return pl.CostEstimate(
        flops=PAIRS * HD * 2 * products, bytes_accessed=16 * MIB, transcendentals=exponentials
    )


def limit(mib):
    return pltpu.CompilerParams(vmem_limit_bytes=mib * MIB)


def bf16(*shape):
    return jax.ShapeDtypeStruct(shape, jnp.bfloat16)


def block_shapes():
    kinds = [jnp.bfloat16, jnp.float32, jnp.bfloat16, jnp.float32]
    return [jax.ShapeDtypeStruct((ROWS, KVH * HD), kind) for kind in kinds]


def probs_and_dv(index, doc_ids, queries, grad_out, keys):
    hbm = pl.BlockSpec(memory_space=pltpu.HBM)
    smem = pl.BlockSpec(memory_space=pltpu.SMEM)
    out = pl.pallas_call(
        probs_kernel,
        in_specs=[smem, VMEM, hbm, hbm] + [VMEM] * 3 + [hbm],
        out_specs=[VMEM] * 7,
        out_shape=[bf16(KVH, SPAN, STACK), bf16(*queries.shape), bf16(KVH, HD, STACK)]
        + block_shapes(),
        scratch_shapes=[
            pltpu.VMEM(grad_out.shape, jnp.bfloat16),
            pltpu.VMEM(keys[3].shape, jnp.bfloat16),
            pltpu.VMEM((SPAN, ROWS), jnp.bfloat16),
            pltpu.SemaphoreType.DMA((2, KVH // GROUPS)),
            pltpu.SemaphoreType.DMA,
        ],
        name="probs_and_dv",
        compiler_params=limit(24),
        cost_estimate=cost(2, PAIRS),
    )(index, doc_ids.reshape(-1, ROWS), queries, grad_out, *keys)
    return out[:3], out[3:]


def dscores_and_dk(q, dot, probs, mark, dv_aside, values):
    out = pl.pallas_call(
        scores_kernel,
        in_specs=[VMEM] * 9,
        out_specs=[VMEM] * 5,
        out_shape=[bf16(KVH, SPAN, STACK), bf16(ROWS, 2 * KVH * HD)] + block_shapes()[1:],
        input_output_aliases={2: 0},
        name="dscores_and_dk",
        compiler_params=limit(24),
        cost_estimate=cost(3),
    )(q, dot, probs, mark, dv_aside, *values)
    return out[0], out[1], out[2:]


def dq_of(dscores, keys, shape):
    return pl.pallas_call(
        queries_kernel,
        grid=(KVH // GROUPS,),
        in_specs=[pl.BlockSpec((GROUPS, SPAN, STACK), lambda s: (s, 0, 0))]
        + [pl.BlockSpec((ROWS, GROUPS * HD), lambda s: (0, s))] * 4,
        out_specs=pl.BlockSpec((ROWS, GROUPS * G * HD), lambda s: (0, s)),
        out_shape=bf16(*shape),
        name="dq",
        compiler_params=limit(24),
        cost_estimate=cost(1),
    )(dscores, *keys)


def place_kernel(index_ref, place_ref):
    place_ref[0] = index_ref[0]


def place_of(index):
    smem = pl.BlockSpec(memory_space=pltpu.SMEM)
    return pl.pallas_call(
        place_kernel,
        in_specs=[smem],
        out_specs=smem,
        out_shape=jax.ShapeDtypeStruct((1,), jnp.int32),
        name="place",
        cost_estimate=pl.CostEstimate(flops=10**11, bytes_accessed=10**8, transcendentals=0),
    )(index.astype(jnp.int32)[None])


def mark_kernel(docs_ref, mark_ref):
    mark_ref[...] = docs_ref[0:8, :]


def small_mark(doc_ids):
    return pl.pallas_call(
        mark_kernel,
        grid=(1,),
        in_specs=[pl.BlockSpec((8, ROWS), lambda i: (0, 0))],
        out_specs=pl.BlockSpec((8, ROWS), lambda i: (0, 0)),
        out_shape=jax.ShapeDtypeStruct((8, ROWS), jnp.int32),
        name="mark",
    )(in_hbm(doc_ids.reshape(-1, ROWS)))


def in_hbm(x):
    return pltpu.with_memory_space_constraint(x, pltpu.HBM)


def per_device(queries, keys, values, grad_out, doc_ids):
    devices = lax.axis_size(AXES)
    index = lax.axis_index(AXES)
    ahead = [(i, i + (1 if i % 2 == 0 else 3)) for i in range(devices)]
    ahead = [pair for pair in ahead if pair[1] < devices]
    skip = [(i, i + 2) for i in range(devices - 2)]
    swap = [(i, i ^ 1) for i in range(devices)]
    back = [(b, a) for a, b in ahead]
    unskip = [(b, a) for a, b in skip]

    mark = small_mark(doc_ids)
    key_aside = lax.ppermute(keys, AXES, ahead)
    key_middle = lax.ppermute(keys, AXES, skip)
    mark, late_values = lax.optimization_barrier((mark, values))
    value_aside = lax.ppermute(late_values, AXES, ahead)
    value_middle = lax.ppermute(late_values, AXES, skip)
    key_aside, late_index = lax.optimization_barrier((key_aside, index))
    place = place_of(late_index)
    key_blocks = [key_aside, key_middle, lax.ppermute(key_middle, AXES, swap), in_hbm(keys)]
    (probs, query_copy, dot), dv_blocks = probs_and_dv(
        place, doc_ids, in_hbm(queries), in_hbm(grad_out), key_blocks
    )
    dv_aside, dv_middle, dv_paired, dv_own = dv_blocks
    _, value_aside, value_middle = lax.optimization_barrier(
        (dv_paired, value_aside, value_middle)
    )
    value_paired = lax.ppermute(value_middle, AXES, swap)
    dv_other = lax.ppermute(dv_paired, AXES, swap)
    dv_far = lax.ppermute((dv_middle + dv_other).astype(jnp.bfloat16), AXES, unskip)
    dscores, aside, dk_blocks = dscores_and_dk(
        query_copy,
        dot,
        probs,
        mark,
        dv_aside,
        [value_aside, value_middle, value_paired, values],
    )
    dk_middle, dk_paired, dk_own = dk_blocks
    dk_paired, dv_far = lax.optimization_barrier((dk_paired, dv_far))
    dk_other = lax.ppermute(dk_paired, AXES, swap)
    near = lax.ppermute(aside, AXES, back)
    dk_far = lax.ppermute((dk_middle + dk_other).astype(jnp.bfloat16), AXES, unskip)
    grad_queries = dq_of(dscores, key_blocks, queries.shape)
    width = keys.shape[1]
    grad_keys = (dk_own + near[:, :width] + dk_far).astype(jnp.bfloat16)
    grad_values = (dv_own + near[:, width:] + dv_far).astype(jnp.bfloat16)
    return grad_queries, grad_keys, grad_values


def solution(mesh):
    split = P(AXES, None)
    return jax.shard_map(
        per_device,
        mesh=mesh,
        in_specs=(split, split, split, split, P()),
        out_specs=(split, split, split),
        check_vma=False,
    )
```

```python
import jax
import jax.numpy as jnp
from jax import lax
from jax.experimental import pallas as pl
from jax.experimental.pallas import tpu as pltpu
from jax.sharding import PartitionSpec as P

KVH = 8
HD = 128
G = 8
WINDOW = 384
ROWS = 128
SPAN = 4 * ROWS
STACK = G * ROWS
AXES = ("inner", "outer")
SCALE = 1.0 / HD**0.5
SCALE_LOG2 = 1.4426950408889634 / HD**0.5
HIDDEN = -1e30
NT = (((1,), (1,)), ((), ()))
GROUPS = 2
MIB = 2**20
VMEM = pl.BlockSpec(memory_space=pltpu.VMEM)


def head_columns(group):
    return pl.ds(pl.multiple_of(group * HD, HD), HD)


def stacked_blocks(refs, group):
    return jnp.concatenate([ref[:, head_columns(group)] for ref in refs], axis=0)


def heads_of(ref, group):
    return [ref[:, head_columns(group * G + h)] for h in range(G)]


def put_blocks(refs, group, value):
    for i, ref in enumerate(refs):
        ref[:, head_columns(group)] = value[i * ROWS : (i + 1) * ROWS].astype(ref.dtype)


def put_bias(index, docs_ref, bias_ref):
    odd = lax.rem(index, 2)
    line = lax.broadcasted_iota(jnp.int32, (ROWS, ROWS), 0)
    lane = lax.broadcasted_iota(jnp.int32, (ROWS, ROWS), 1)

    def docs_of(block):
        row = docs_ref[pl.ds(jnp.maximum(block, 0), 1), :].astype(jnp.float32)
        return jnp.broadcast_to(row, (ROWS, ROWS))

    query_doc = docs_of(index)
    for i, offset in enumerate([3 - 2 * odd, 2, 1 + 2 * odd, 0]):
        gap = offset * ROWS + lane - line
        same = docs_of(index - offset).T == query_doc
        visible = (gap >= 0) & (gap < WINDOW) & (index >= offset) & same
        bias_ref[i * ROWS : (i + 1) * ROWS] = jnp.where(visible, 0.0, HIDDEN).astype(jnp.bfloat16)


def stack_kernel(index_ref, docs_ref, query_hbm, dout_hbm, keys_hbm, *refs):
    qt_ref, dot_ref, query_ref, dout_ref, bias_ref, own_ref, sems, own_sem = refs
    loads = []
    for i, (source, target) in enumerate([(query_hbm, query_ref), (dout_hbm, dout_ref)]):
        for g in range(KVH):
            part = slice(g * STACK, (g + 1) * STACK)
            loads.append(
                pltpu.make_async_copy(source.at[:, part], target.at[:, part], sems.at[i, g])
            )
    own_load = pltpu.make_async_copy(keys_hbm, own_ref, own_sem)
    for load in [*loads, own_load]:
        load.start()
    put_bias(index_ref[0], docs_ref, bias_ref)
    for g in range(KVH):
        loads[g].wait()
        loads[KVH + g].wait()
        for source, target in [(query_ref, qt_ref), (dout_ref, dot_ref)]:
            target[g] = jnp.concatenate([head.T for head in heads_of(source, g)], axis=1)
    own_load.wait()


def probs_kernel(place_ref, qt_ref, bias_ref, dout_ref, *refs):
    key_refs, probs_ref, dv_refs = refs[:4], refs[4], refs[5:9]
    bias = bias_ref[...]
    row = lax.broadcasted_iota(jnp.int32, (ROWS, STACK), 0)
    column = lax.broadcasted_iota(jnp.int32, (ROWS, STACK), 1)
    identity = jnp.where((column & (ROWS - 1)) == row, 1.0, 0.0).astype(jnp.bfloat16)

    def step(i, carry):
        groups = [i * GROUPS + j for j in range(GROUPS)]
        scores = [
            jnp.dot(
                jnp.concatenate([stacked_blocks(key_refs, g), bias], axis=1),
                jnp.concatenate([qt_ref[g], identity], axis=0),
                preferred_element_type=jnp.float32,
            )
            for g in groups
        ]
        for g, score in zip(groups, scores):
            powers = jnp.exp2((score - jnp.max(score, axis=0, keepdims=True)) * SCALE_LOG2)
            probs = powers * (1.0 / jnp.sum(powers, axis=0, keepdims=True))
            probs_b = probs.astype(jnp.bfloat16)
            probs_ref[g] = probs_b
            dout = jnp.concatenate(heads_of(dout_ref, g), axis=0)
            put_blocks(dv_refs, g, jnp.dot(probs_b, dout, preferred_element_type=jnp.float32))
        return carry

    lax.fori_loop(0, KVH // GROUPS, step, 0)


def scores_kernel(query_ref, dot_ref, probs_ref, *refs):
    value_refs, dscores_ref, dk_refs = refs[:4], refs[4], refs[5:9]
    def step(i, carry):
        groups = [i * GROUPS + j for j in range(GROUPS)]
        deltas, dprobs = [], []
        for g in groups:
            values = stacked_blocks(value_refs, g)
            out = jnp.dot(values.T, probs_ref[g], preferred_element_type=jnp.float32)
            out = out.astype(jnp.bfloat16).astype(jnp.float32)
            deltas.append(jnp.sum(out * dot_ref[g].astype(jnp.float32), axis=0, keepdims=True))
            dprobs.append(jnp.dot(values, dot_ref[g], preferred_element_type=jnp.float32))
        for g, delta, dprob in zip(groups, deltas, dprobs):
            dscores = (probs_ref[g].astype(jnp.float32) * (dprob - delta)).astype(jnp.bfloat16)
            dscores_ref[g] = dscores
            query = jnp.concatenate(heads_of(query_ref, g), axis=0)
            dk = jnp.dot(dscores, query, preferred_element_type=jnp.float32)
            put_blocks(dk_refs, g, dk * SCALE)
        return carry

    lax.fori_loop(0, KVH // GROUPS, step, 0)


def queries_kernel(dscores_ref, *refs):
    key_refs, dq_ref = refs[:4], refs[4]
    for g in range(GROUPS):
        keys = jnp.concatenate([ref[:, g * HD : (g + 1) * HD] for ref in key_refs], axis=0)
        dq = jnp.dot(keys.T, dscores_ref[g], preferred_element_type=jnp.float32) * SCALE
        for h in range(G):
            column = (g * G + h) * HD
            dq_ref[:, column : column + HD] = dq[:, h * HD : (h + 1) * HD].T.astype(dq_ref.dtype)


PAIRS = KVH * G * SPAN * ROWS


def cost(products, exponentials=0):
    return pl.CostEstimate(
        flops=PAIRS * HD * 2 * products, bytes_accessed=16 * MIB, transcendentals=exponentials
    )


def limit(mib):
    return pltpu.CompilerParams(vmem_limit_bytes=mib * MIB)


def bf16(*shape):
    return jax.ShapeDtypeStruct(shape, jnp.bfloat16)


def block_shapes():
    kinds = [jnp.bfloat16, jnp.float32, jnp.bfloat16, jnp.float32]
    return [jax.ShapeDtypeStruct((ROWS, KVH * HD), kind) for kind in kinds]


HBM = pl.BlockSpec(memory_space=pltpu.HBM)
SMEM = pl.BlockSpec(memory_space=pltpu.SMEM)


def stacked(index, doc_ids, queries, grad_out, keys):
    flat = (KVH, HD, STACK)
    return pl.pallas_call(
        stack_kernel,
        in_specs=[SMEM, VMEM, HBM, HBM, HBM],
        out_specs=[VMEM] * 6,
        out_shape=[
            pltpu.VMEM(shape, jnp.bfloat16)
            for shape in (flat, flat, queries.shape, queries.shape, (SPAN, ROWS), keys.shape)
        ],
        scratch_shapes=[
            pltpu.SemaphoreType.DMA((2, KVH)),
            pltpu.SemaphoreType.DMA,
        ],
        name="stacked",
        compiler_params=limit(12),
    )(index.astype(jnp.int32)[None], doc_ids.reshape(-1, ROWS), queries, grad_out, keys)


def probs_and_dv(place, qt, bias, grad_out, keys):
    out = pl.pallas_call(
        probs_kernel,
        in_specs=[SMEM] + [VMEM] * 7,
        out_specs=[VMEM] * 5,
        out_shape=[bf16(KVH, SPAN, STACK)] + block_shapes(),
        name="probs_and_dv",
        compiler_params=limit(10),
        cost_estimate=cost(2, PAIRS),
    )(place, qt, bias, grad_out, *keys)
    return out[0], out[1:]


def dscores_and_dk(queries, dot, probs, values):
    out = pl.pallas_call(
        scores_kernel,
        in_specs=[VMEM] * 7,
        out_specs=[VMEM] * 5,
        out_shape=[bf16(KVH, SPAN, STACK)] + block_shapes(),
        input_output_aliases={2: 0},
        name="dscores_and_dk",
        compiler_params=limit(10),
        cost_estimate=cost(3),
    )(queries, dot, probs, *values)
    return out[0], out[1:]


def dq_of(dscores, keys, shape):
    return pl.pallas_call(
        queries_kernel,
        grid=(KVH // GROUPS,),
        in_specs=[pl.BlockSpec((GROUPS, SPAN, STACK), lambda s: (s, 0, 0))]
        + [pl.BlockSpec((ROWS, GROUPS * HD), lambda s: (0, s))] * 4,
        out_specs=pl.BlockSpec((ROWS, GROUPS * G * HD), lambda s: (0, s)),
        out_shape=bf16(*shape),
        name="dq",
        compiler_params=limit(24),
        cost_estimate=cost(1),
    )(dscores, *keys)


def place_kernel(index_ref, place_ref):
    place_ref[0] = index_ref[0]


def place_of(index):
    smem = pl.BlockSpec(memory_space=pltpu.SMEM)
    return pl.pallas_call(
        place_kernel,
        in_specs=[smem],
        out_specs=smem,
        out_shape=jax.ShapeDtypeStruct((1,), jnp.int32),
        name="place",
        compiler_params=limit(1),
        cost_estimate=pl.CostEstimate(flops=10**11, bytes_accessed=10**8, transcendentals=0),
    )(index.astype(jnp.int32)[None])


def sum_kernel(place_ref, own_ref, other_ref, out_ref):
    out_ref[...] = (own_ref[...] + other_ref[...].astype(jnp.float32)).astype(jnp.bfloat16)


def sum_of(place, own, other):
    return pl.pallas_call(
        sum_kernel,
        in_specs=[SMEM, VMEM, VMEM],
        out_specs=VMEM,
        out_shape=pltpu.VMEM(own.shape, jnp.bfloat16),
        name="sum",
        compiler_params=limit(2),
    )(place, own, other)


def in_hbm(x):
    return pltpu.with_memory_space_constraint(x, pltpu.HBM)


def per_device(queries, keys, values, grad_out, doc_ids):
    devices = lax.axis_size(AXES)
    index = lax.axis_index(AXES)
    ahead = [(i, i + (1 if i % 2 == 0 else 3)) for i in range(devices)]
    ahead = [pair for pair in ahead if pair[1] < devices]
    skip = [(i, i + 2) for i in range(devices - 2)]
    swap = [(i, i ^ 1) for i in range(devices)]
    back = [(b, a) for a, b in ahead]
    unskip = [(b, a) for a, b in skip]

    queries, grad_out = in_hbm(queries), in_hbm(grad_out)
    key_aside = lax.ppermute(keys, AXES, ahead)
    key_middle = lax.ppermute(keys, AXES, skip)
    qt, dot, queries, grad_out, bias, own_keys = stacked(index, doc_ids, queries, grad_out, in_hbm(keys))
    dot, queries, late_values = lax.optimization_barrier((dot, queries, values))
    value_aside = lax.ppermute(late_values, AXES, ahead)
    value_middle = lax.ppermute(late_values, AXES, skip)
    key_paired = lax.ppermute(key_middle, AXES, swap)
    key_aside, key_middle, late_index, qt, grad_out, bias, own_keys = lax.optimization_barrier(
        (key_aside, key_middle, index, qt, grad_out, bias, own_keys)
    )
    place = place_of(late_index)
    key_blocks = [key_aside, key_middle, key_paired, own_keys]
    probs, dv_blocks = probs_and_dv(place, qt, bias, grad_out, key_blocks)
    dv_aside, dv_middle, dv_paired, dv_own = dv_blocks
    _, value_aside, value_middle = lax.optimization_barrier(
        (dv_paired, value_aside, value_middle)
    )
    value_paired = lax.ppermute(value_middle, AXES, swap)
    dv_other = lax.ppermute(dv_paired, AXES, swap)
    dv_far = lax.ppermute((dv_middle + dv_other).astype(jnp.bfloat16), AXES, unskip)
    dv_near = lax.ppermute(dv_aside, AXES, back)
    dscores, dk_blocks = dscores_and_dk(
        queries,
        dot,
        probs,
        [value_aside, value_middle, value_paired, values],
    )
    dk_aside, dk_middle, dk_paired, dk_own = dk_blocks

    dk_other = lax.ppermute(dk_paired, AXES, swap)
    dk_near = lax.ppermute(dk_aside, AXES, back)
    dk_middle, late_index = lax.optimization_barrier((dk_middle, index))
    dk_sum = sum_of(place_of(late_index), dk_middle, dk_other)
    dk_far = lax.ppermute(dk_sum, AXES, unskip)
    grad_queries = dq_of(dscores, key_blocks, queries.shape)
    grad_keys = (dk_own + dk_near + dk_far).astype(jnp.bfloat16)
    grad_values = (dv_own + dv_near + dv_far).astype(jnp.bfloat16)
    return grad_queries, grad_keys, grad_values


def solution(mesh):
    split = P(AXES, None)
    return jax.shard_map(
        per_device,
        mesh=mesh,
        in_specs=(split, split, split, split, P()),
        out_specs=(split, split, split),
        check_vma=False,
    )
```

```python
import jax
import jax.numpy as jnp
from jax import lax
from jax.experimental import pallas as pl
from jax.experimental.pallas import tpu as pltpu
from jax.sharding import PartitionSpec as P

KVH = 8
HD = 128
G = 8
WINDOW = 384
ROWS = 128
SPAN = 4 * ROWS
STACK = G * ROWS
AXES = ("inner", "outer")
SCALE = 1.0 / HD**0.5
SCALE_LOG2 = 1.4426950408889634 / HD**0.5
HIDDEN = -1e30
KEY_MOST = 6.0
NT = (((1,), (1,)), ((), ()))
GROUPS = 2
MIB = 2**20
VMEM = pl.BlockSpec(memory_space=pltpu.VMEM)


def head_columns(group):
    return pl.ds(pl.multiple_of(group * HD, HD), HD)


def stacked_blocks(refs, group):
    return jnp.concatenate([ref[:, head_columns(group)] for ref in refs], axis=0)


def heads_of(ref, group):
    return [ref[:, head_columns(group * G + h)] for h in range(G)]


def put_blocks(refs, group, value):
    for i, ref in enumerate(refs):
        ref[:, head_columns(group)] = value[i * ROWS : (i + 1) * ROWS].astype(ref.dtype)


def put_bias(index, docs_ref, bias_ref):
    odd = lax.rem(index, 2)
    line = lax.broadcasted_iota(jnp.int32, (ROWS, ROWS), 0)
    lane = lax.broadcasted_iota(jnp.int32, (ROWS, ROWS), 1)

    def docs_of(block):
        row = docs_ref[pl.ds(jnp.maximum(block, 0), 1), :].astype(jnp.float32)
        return jnp.broadcast_to(row, (ROWS, ROWS))

    query_doc = docs_of(index)
    for i, offset in enumerate([3 - 2 * odd, 2, 1 + 2 * odd, 0]):
        gap = offset * ROWS + lane - line
        same = docs_of(index - offset).T == query_doc
        visible = (gap >= 0) & (gap < WINDOW) & (index >= offset) & same
        bias_ref[i * ROWS : (i + 1) * ROWS] = jnp.where(visible, 0.0, HIDDEN).astype(jnp.bfloat16)


def stack_kernel(index_ref, docs_hbm, query_hbm, dout_hbm, keys_hbm, *refs):
    qt_ref, dot_ref, query_ref, dout_ref, bias_ref, own_ref, size_ref = refs[:7]
    docs_ref, sems, own_sem, docs_sem = refs[7:]
    loads = []
    for i, (source, target) in enumerate([(query_hbm, query_ref), (dout_hbm, dout_ref)]):
        for g in range(KVH):
            part = slice(g * STACK, (g + 1) * STACK)
            loads.append(
                pltpu.make_async_copy(source.at[:, part], target.at[:, part], sems.at[i, g])
            )
    own_load = pltpu.make_async_copy(keys_hbm, own_ref, own_sem)
    docs_load = pltpu.make_async_copy(docs_hbm, docs_ref, docs_sem)
    for load in [docs_load, *loads, own_load]:
        load.start()
    docs_load.wait()
    put_bias(index_ref[0], docs_ref, bias_ref)
    size = jnp.zeros((1, STACK), jnp.float32)
    for g in range(KVH):
        loads[g].wait()
        loads[KVH + g].wait()
        for source, target in [(query_ref, qt_ref), (dout_ref, dot_ref)]:
            target[g] = jnp.concatenate([head.T for head in heads_of(source, g)], axis=1)
        sums = jnp.sum(jnp.abs(qt_ref[g].astype(jnp.float32)), axis=0, keepdims=True)
        size = jnp.maximum(size, sums)
    size_ref[...] = jnp.broadcast_to(size, size_ref.shape)
    own_load.wait()


def probs_kernel(place_ref, size_ref, qt_ref, bias_ref, dout_ref, *refs):
    key_refs, probs_ref, dv_refs = refs[:4], refs[4], refs[5:9]
    bias = bias_ref[...]
    row = lax.broadcasted_iota(jnp.int32, (ROWS, STACK), 0)
    column = lax.broadcasted_iota(jnp.int32, (ROWS, STACK), 1)
    identity = jnp.where((column & (ROWS - 1)) == row, 1.0, 0.0).astype(jnp.bfloat16)

    def step(i, shift):
        groups = [i * GROUPS + j for j in range(GROUPS)]
        scores = [
            jnp.dot(
                jnp.concatenate([stacked_blocks(key_refs, g), bias], axis=1),
                jnp.concatenate([qt_ref[g], identity], axis=0),
                preferred_element_type=jnp.float32,
            )
            for g in groups
        ]
        for g, score in zip(groups, scores):
            if shift:
                score = score - jnp.max(score, axis=0, keepdims=True)
            powers = jnp.exp2(score * SCALE_LOG2)
            probs = powers * (1.0 / jnp.sum(powers, axis=0, keepdims=True))
            probs_b = probs.astype(jnp.bfloat16)
            probs_ref[g] = probs_b
            dout = jnp.concatenate(heads_of(dout_ref, g), axis=0)
            put_blocks(dv_refs, g, jnp.dot(probs_b, dout, preferred_element_type=jnp.float32))

    def run(shift):
        def body(i, carry):
            step(i, shift)
            return carry

        lax.fori_loop(0, KVH // GROUPS, body, 0)

    small = jnp.max(size_ref[0:1]) * (KEY_MOST * SCALE_LOG2) <= 115.0
    pl.when(small)(lambda: run(False))
    pl.when(jnp.logical_not(small))(lambda: run(True))


def scores_kernel(mark_ref, query_ref, dot_ref, probs_ref, *refs):
    value_refs, dscores_ref, dk_refs = refs[:4], refs[4], refs[5:9]
    def step(i, carry):
        groups = [i * GROUPS + j for j in range(GROUPS)]
        deltas, dprobs = [], []
        for g in groups:
            values = stacked_blocks(value_refs, g)
            out = jnp.dot(values.T, probs_ref[g], preferred_element_type=jnp.float32)
            out = out.astype(jnp.bfloat16).astype(jnp.float32)
            deltas.append(jnp.sum(out * dot_ref[g].astype(jnp.float32), axis=0, keepdims=True))
            dprobs.append(jnp.dot(values, dot_ref[g], preferred_element_type=jnp.float32))
        for g, delta, dprob in zip(groups, deltas, dprobs):
            dscores = (probs_ref[g].astype(jnp.float32) * (dprob - delta)).astype(jnp.bfloat16)
            dscores_ref[g] = dscores
            query = jnp.concatenate(heads_of(query_ref, g), axis=0)
            dk = jnp.dot(dscores, query, preferred_element_type=jnp.float32)
            put_blocks(dk_refs, g, dk * SCALE)
        return carry

    lax.fori_loop(0, KVH // GROUPS, step, 0)


def queries_kernel(dscores_ref, *refs):
    key_refs, dq_ref = refs[:4], refs[-1]
    for g in range(GROUPS):
        keys = jnp.concatenate([ref[:, g * HD : (g + 1) * HD] for ref in key_refs], axis=0)
        dq = jnp.dot(keys.T, dscores_ref[g], preferred_element_type=jnp.float32) * SCALE
        for h in range(G):
            column = (g * G + h) * HD
            dq_ref[:, column : column + HD] = dq[:, h * HD : (h + 1) * HD].T.astype(dq_ref.dtype)


PAIRS = KVH * G * SPAN * ROWS


def cost(products, exponentials=0):
    return pl.CostEstimate(
        flops=PAIRS * HD * 2 * products, bytes_accessed=16 * MIB, transcendentals=exponentials
    )


AHEAD = pl.CostEstimate(flops=10**11, bytes_accessed=10**8, transcendentals=0)


def limit(mib):
    return pltpu.CompilerParams(vmem_limit_bytes=mib * MIB)


def bf16(*shape):
    return jax.ShapeDtypeStruct(shape, jnp.bfloat16)


def block_shapes():
    kinds = [jnp.bfloat16, jnp.float32, jnp.bfloat16, jnp.float32]
    return [jax.ShapeDtypeStruct((ROWS, KVH * HD), kind) for kind in kinds]


HBM = pl.BlockSpec(memory_space=pltpu.HBM)
SMEM = pl.BlockSpec(memory_space=pltpu.SMEM)


def stacked(index, doc_ids, queries, grad_out, keys):
    flat = (KVH, HD, STACK)
    return pl.pallas_call(
        stack_kernel,
        in_specs=[SMEM, HBM, HBM, HBM, HBM],
        out_specs=[VMEM] * 7,
        out_shape=[
            pltpu.VMEM(shape, jnp.bfloat16)
            for shape in (flat, flat, queries.shape, queries.shape, (SPAN, ROWS), keys.shape)
        ]
        + [pltpu.VMEM((8, STACK), jnp.float32)],
        scratch_shapes=[
            pltpu.VMEM((doc_ids.shape[0] // ROWS, ROWS), jnp.int32),
            pltpu.SemaphoreType.DMA((2, KVH)),
            pltpu.SemaphoreType.DMA,
            pltpu.SemaphoreType.DMA,
        ],
        name="stacked",
        compiler_params=limit(12),
    )(index.astype(jnp.int32)[None], in_hbm(doc_ids.reshape(-1, ROWS)), queries, grad_out, keys)


def probs_and_dv(place, size, qt, bias, grad_out, keys):
    out = pl.pallas_call(
        probs_kernel,
        in_specs=[SMEM] + [VMEM] * 8,
        out_specs=[VMEM] * 5,
        out_shape=[bf16(KVH, SPAN, STACK)] + block_shapes(),
        name="probs_and_dv",
        compiler_params=limit(10),
        cost_estimate=cost(2, PAIRS),
    )(place, size, qt, bias, grad_out, *keys)
    return out[0], out[1:]


def dscores_and_dk(mark, queries, dot, probs, values):
    out = pl.pallas_call(
        scores_kernel,
        in_specs=[SMEM] + [VMEM] * 7,
        out_specs=[VMEM] * 5,
        out_shape=[bf16(KVH, SPAN, STACK)] + block_shapes(),
        input_output_aliases={3: 0},
        name="dscores_and_dk",
        compiler_params=limit(10),
        cost_estimate=cost(3),
    )(mark, queries, dot, probs, *values)
    return out[0], out[1:]


def dq_of(dscores, keys, shape, first, count, earlier=()):
    return pl.pallas_call(
        queries_kernel,
        grid=(count,),
        in_specs=[pl.BlockSpec((GROUPS, SPAN, STACK), lambda s: (s + first, 0, 0))]
        + [pl.BlockSpec((ROWS, GROUPS * HD), lambda s: (0, s + first))] * 4
        + [pl.BlockSpec(memory_space=pl.ANY)] * len(earlier),
        out_specs=pl.BlockSpec((ROWS, GROUPS * G * HD), lambda s: (0, s + first)),
        out_shape=bf16(*shape),
        input_output_aliases={5: 0} if earlier else {},
        name="dq",
        compiler_params=limit(24),
        cost_estimate=cost(1) if earlier else AHEAD,
    )(dscores, *keys, *earlier)


def place_kernel(index_ref, place_ref):
    place_ref[0] = index_ref[0]


def mark_of(index):
    smem = pl.BlockSpec(memory_space=pltpu.SMEM)
    return pl.pallas_call(
        place_kernel,
        in_specs=[smem],
        out_specs=smem,
        out_shape=jax.ShapeDtypeStruct((1,), jnp.int32),
        name="mark",
        compiler_params=limit(1),
    )(index.astype(jnp.int32)[None])


def place_of(index):
    smem = pl.BlockSpec(memory_space=pltpu.SMEM)
    return pl.pallas_call(
        place_kernel,
        in_specs=[smem],
        out_specs=smem,
        out_shape=jax.ShapeDtypeStruct((1,), jnp.int32),
        name="place",
        compiler_params=limit(1),
        cost_estimate=AHEAD,
    )(index.astype(jnp.int32)[None])


def in_hbm(x):
    return pltpu.with_memory_space_constraint(x, pltpu.HBM)


def per_device(queries, keys, values, grad_out, doc_ids):
    devices = lax.axis_size(AXES)
    index = lax.axis_index(AXES)
    ahead = [(i, i + (1 if i % 2 == 0 else 3)) for i in range(devices)]
    ahead = [pair for pair in ahead if pair[1] < devices]
    skip = [(i, i + 2) for i in range(devices - 2)]
    swap = [(i, i ^ 1) for i in range(devices)]
    back = [(b, a) for a, b in ahead]
    unskip = [(b, a) for a, b in skip]

    queries, grad_out = in_hbm(queries), in_hbm(grad_out)
    key_aside = lax.ppermute(keys, AXES, ahead)
    key_middle = lax.ppermute(keys, AXES, skip)
    qt, dot, queries, grad_out, bias, own_keys, size = stacked(index, doc_ids, queries, grad_out, in_hbm(keys))
    mark, late_values = lax.optimization_barrier((mark_of(index), values))
    value_aside = lax.ppermute(late_values, AXES, ahead)
    value_middle = lax.ppermute(late_values, AXES, skip)
    key_paired = lax.ppermute(key_middle, AXES, swap)
    key_aside, key_middle, late_index, qt, grad_out, bias, own_keys, size = lax.optimization_barrier(
        (key_aside, key_middle, index, qt, grad_out, bias, own_keys, size)
    )
    place = place_of(late_index)
    key_blocks = [key_aside, key_middle, key_paired, own_keys]
    probs, dv_blocks = probs_and_dv(place, size, qt, bias, grad_out, key_blocks)
    dv_aside, dv_middle, dv_paired, dv_own = dv_blocks
    _, value_aside, value_middle = lax.optimization_barrier(
        (dv_paired, value_aside, value_middle)
    )
    value_paired = lax.ppermute(value_middle, AXES, swap)
    dv_other = lax.ppermute(dv_paired, AXES, swap)
    dv_far = lax.ppermute((dv_middle + dv_other).astype(jnp.bfloat16), AXES, unskip)
    dv_near = lax.ppermute(dv_aside, AXES, back)
    dscores, dk_blocks = dscores_and_dk(
        mark,
        queries,
        dot,
        probs,
        [value_aside, value_middle, value_paired, values],
    )
    dk_aside, dk_middle, dk_paired, dk_own = dk_blocks

    dk_other = lax.ppermute(dk_paired, AXES, swap)
    first_dq = dq_of(dscores, key_blocks, queries.shape, 0, 1)
    dk_other, first_dq = lax.optimization_barrier((dk_other, first_dq))
    dk_sum = (dk_middle + dk_other).astype(jnp.bfloat16)
    dk_far = lax.ppermute(dk_sum, AXES, unskip)
    dk_sum, dk_aside = lax.optimization_barrier((dk_sum, dk_aside))
    dk_near = lax.ppermute(dk_aside, AXES, back)
    grad_queries = dq_of(dscores, key_blocks, queries.shape, 1, KVH // GROUPS - 1, [first_dq])
    grad_keys = (dk_own + dk_near + dk_far).astype(jnp.bfloat16)
    grad_values = (dv_own + dv_near + dv_far).astype(jnp.bfloat16)
    return grad_queries, grad_keys, grad_values


def solution(mesh):
    split = P(AXES, None)
    return jax.shard_map(
        per_device,
        mesh=mesh,
        in_specs=(split, split, split, split, P()),
        out_specs=(split, split, split),
        check_vma=False,
    )
```

```python
import jax
import jax.numpy as jnp
from jax import lax
from jax.experimental import pallas as pl
from jax.experimental.pallas import tpu as pltpu
from jax.sharding import PartitionSpec as P

KVH = 8
HD = 128
G = 8
WINDOW = 384
ROWS = 128
SPAN = 4 * ROWS
STACK = G * ROWS
AXES = ("inner", "outer")
SCALE = 1.0 / HD**0.5
SCALE_LOG2 = 1.4426950408889634 / HD**0.5
HIDDEN = -1e30
KEY_MOST = 6.0
NT = (((1,), (1,)), ((), ()))
GROUPS = 2
MIB = 2**20
VMEM = pl.BlockSpec(memory_space=pltpu.VMEM)


def head_columns(group):
    return pl.ds(pl.multiple_of(group * HD, HD), HD)


def stacked_blocks(refs, group):
    return jnp.concatenate([ref[:, head_columns(group)] for ref in refs], axis=0)


def heads_of(ref, group):
    return [ref[:, head_columns(group * G + h)] for h in range(G)]


def put_blocks(refs, group, value):
    for i, ref in enumerate(refs):
        ref[:, head_columns(group)] = value[i * ROWS : (i + 1) * ROWS].astype(ref.dtype)


def put_bias(index, docs_ref, bias_ref):
    odd = lax.rem(index, 2)
    line = lax.broadcasted_iota(jnp.int32, (ROWS, ROWS), 0)
    lane = lax.broadcasted_iota(jnp.int32, (ROWS, ROWS), 1)

    def docs_of(block):
        row = docs_ref[pl.ds(jnp.maximum(block, 0), 1), :].astype(jnp.float32)
        return jnp.broadcast_to(row, (ROWS, ROWS))

    query_doc = docs_of(index)
    for i, offset in enumerate([3 - 2 * odd, 2, 1 + 2 * odd, 0]):
        gap = offset * ROWS + lane - line
        same = docs_of(index - offset).T == query_doc
        visible = (gap >= 0) & (gap < WINDOW) & (index >= offset) & same
        bias_ref[i * ROWS : (i + 1) * ROWS] = jnp.where(visible, 0.0, HIDDEN).astype(jnp.bfloat16)


def stack_kernel(docs_hbm, query_hbm, dout_hbm, keys_hbm, *refs):
    qt_ref, dot_ref, query_ref, dout_ref, bias_ref, own_ref, size_ref = refs[:7]
    docs_ref, sems, own_sem, docs_sem = refs[7:]
    loads = []
    for i, (source, target) in enumerate([(query_hbm, query_ref), (dout_hbm, dout_ref)]):
        for g in range(KVH):
            part = slice(g * STACK, (g + 1) * STACK)
            loads.append(
                pltpu.make_async_copy(source.at[:, part], target.at[:, part], sems.at[i, g])
            )
    own_load = pltpu.make_async_copy(keys_hbm, own_ref, own_sem)
    docs_load = pltpu.make_async_copy(docs_hbm, docs_ref, docs_sem)
    for load in [docs_load, *loads, own_load]:
        load.start()
    docs_load.wait()
    put_bias(lax.axis_index(AXES), docs_ref, bias_ref)
    size = jnp.zeros((1, STACK), jnp.float32)
    for g in range(KVH):
        loads[g].wait()
        loads[KVH + g].wait()
        for source, target in [(query_ref, qt_ref), (dout_ref, dot_ref)]:
            target[g] = jnp.concatenate([head.T for head in heads_of(source, g)], axis=1)
        sums = jnp.sum(jnp.abs(qt_ref[g].astype(jnp.float32)), axis=0, keepdims=True)
        size = jnp.maximum(size, sums)
    size_ref[...] = jnp.broadcast_to(size, size_ref.shape)
    own_load.wait()


def probs_kernel(size_ref, qt_ref, bias_ref, dout_ref, *refs):
    key_refs, probs_ref, dv_refs = refs[:4], refs[4], refs[5:9]
    bias = bias_ref[...]
    row = lax.broadcasted_iota(jnp.int32, (ROWS, STACK), 0)
    column = lax.broadcasted_iota(jnp.int32, (ROWS, STACK), 1)
    identity = jnp.where((column & (ROWS - 1)) == row, 1.0, 0.0).astype(jnp.bfloat16)

    def step(i, shift):
        groups = [i * GROUPS + j for j in range(GROUPS)]
        scores = [
            jnp.dot(
                jnp.concatenate([stacked_blocks(key_refs, g), bias], axis=1),
                jnp.concatenate([qt_ref[g], identity], axis=0),
                preferred_element_type=jnp.float32,
            )
            for g in groups
        ]
        for g, score in zip(groups, scores):
            if shift:
                score = score - jnp.max(score, axis=0, keepdims=True)
            powers = jnp.exp2(score * SCALE_LOG2)
            probs = powers * (1.0 / jnp.sum(powers, axis=0, keepdims=True))
            probs_b = probs.astype(jnp.bfloat16)
            probs_ref[g] = probs_b
            dout = jnp.concatenate(heads_of(dout_ref, g), axis=0)
            put_blocks(dv_refs, g, jnp.dot(probs_b, dout, preferred_element_type=jnp.float32))

    def run(shift):
        def body(i, carry):
            step(i, shift)
            return carry

        lax.fori_loop(0, KVH // GROUPS, body, 0)

    small = jnp.max(size_ref[0:1]) * (KEY_MOST * SCALE_LOG2) <= 115.0
    pl.when(small)(lambda: run(False))
    pl.when(jnp.logical_not(small))(lambda: run(True))


def scores_kernel(mark_ref, query_ref, dot_ref, probs_ref, *refs):
    value_refs, dscores_ref, dk_refs = refs[:4], refs[4], refs[5:9]
    def step(i, carry):
        groups = [i * GROUPS + j for j in range(GROUPS)]
        deltas, dprobs = [], []
        for g in groups:
            values = stacked_blocks(value_refs, g)
            out = jnp.dot(values.T, probs_ref[g], preferred_element_type=jnp.float32)
            out = out.astype(jnp.bfloat16).astype(jnp.float32)
            deltas.append(jnp.sum(out * dot_ref[g].astype(jnp.float32), axis=0, keepdims=True))
            dprobs.append(jnp.dot(values, dot_ref[g], preferred_element_type=jnp.float32))
        for g, delta, dprob in zip(groups, deltas, dprobs):
            dscores = (probs_ref[g].astype(jnp.float32) * (dprob - delta)).astype(jnp.bfloat16)
            dscores_ref[g] = dscores
            query = jnp.concatenate(heads_of(query_ref, g), axis=0)
            dk = jnp.dot(dscores, query, preferred_element_type=jnp.float32)
            put_blocks(dk_refs, g, dk * SCALE)
        return carry

    lax.fori_loop(0, KVH // GROUPS, step, 0)


def queries_kernel(dscores_ref, *refs):
    key_refs, dq_ref = refs[:4], refs[-1]
    for g in range(GROUPS):
        keys = jnp.concatenate([ref[:, g * HD : (g + 1) * HD] for ref in key_refs], axis=0)
        dq = jnp.dot(keys.T, dscores_ref[g], preferred_element_type=jnp.float32) * SCALE
        for h in range(G):
            column = (g * G + h) * HD
            dq_ref[:, column : column + HD] = dq[:, h * HD : (h + 1) * HD].T.astype(dq_ref.dtype)


PAIRS = KVH * G * SPAN * ROWS


def cost(products, exponentials=0):
    return pl.CostEstimate(
        flops=PAIRS * HD * 2 * products, bytes_accessed=16 * MIB, transcendentals=exponentials
    )


AHEAD = pl.CostEstimate(flops=10**11, bytes_accessed=10**8, transcendentals=0)


def limit(mib):
    return pltpu.CompilerParams(vmem_limit_bytes=mib * MIB)


def bf16(*shape):
    return jax.ShapeDtypeStruct(shape, jnp.bfloat16)


def block_shapes():
    kinds = [jnp.bfloat16, jnp.float32, jnp.bfloat16, jnp.float32]
    return [jax.ShapeDtypeStruct((ROWS, KVH * HD), kind) for kind in kinds]


HBM = pl.BlockSpec(memory_space=pltpu.HBM)


def stacked(doc_ids, queries, grad_out, keys):
    flat = (KVH, HD, STACK)
    return pl.pallas_call(
        stack_kernel,
        in_specs=[HBM, HBM, HBM, HBM],
        out_specs=[VMEM] * 7,
        out_shape=[
            pltpu.VMEM(shape, jnp.bfloat16)
            for shape in (flat, flat, queries.shape, queries.shape, (SPAN, ROWS), keys.shape)
        ]
        + [pltpu.VMEM((8, STACK), jnp.float32)],
        scratch_shapes=[
            pltpu.VMEM((doc_ids.shape[0] // ROWS, ROWS), jnp.int32),
            pltpu.SemaphoreType.DMA((2, KVH)),
            pltpu.SemaphoreType.DMA,
            pltpu.SemaphoreType.DMA,
        ],
        name="stacked",
        compiler_params=limit(12),
    )(in_hbm(doc_ids.reshape(-1, ROWS)), queries, grad_out, keys)


def probs_and_dv(size, qt, bias, grad_out, keys):
    out = pl.pallas_call(
        probs_kernel,
        in_specs=[VMEM] * 8,
        out_specs=[VMEM] * 5,
        out_shape=[bf16(KVH, SPAN, STACK)] + block_shapes(),
        name="probs_and_dv",
        compiler_params=limit(10),
        cost_estimate=cost(2, PAIRS),
    )(size, qt, bias, grad_out, *keys)
    return out[0], out[1:]


def dscores_and_dk(mark, queries, dot, probs, values):
    out = pl.pallas_call(
        scores_kernel,
        in_specs=[VMEM] * 8,
        out_specs=[VMEM] * 5,
        out_shape=[bf16(KVH, SPAN, STACK)] + block_shapes(),
        input_output_aliases={3: 0},
        name="dscores_and_dk",
        compiler_params=limit(10),
        cost_estimate=cost(3),
    )(mark, queries, dot, probs, *values)
    return out[0], out[1:]


def dq_of(dscores, keys, shape, first, count, earlier=()):
    return pl.pallas_call(
        queries_kernel,
        grid=(count,),
        in_specs=[pl.BlockSpec((GROUPS, SPAN, STACK), lambda s: (s + first, 0, 0))]
        + [pl.BlockSpec((ROWS, GROUPS * HD), lambda s: (0, s + first))] * 4
        + [pl.BlockSpec(memory_space=pl.ANY)] * len(earlier),
        out_specs=pl.BlockSpec((ROWS, GROUPS * G * HD), lambda s: (0, s + first)),
        out_shape=bf16(*shape),
        input_output_aliases={5: 0} if earlier else {},
        name="dq",
        compiler_params=limit(24),
        cost_estimate=cost(1) if earlier else AHEAD,
    )(dscores, *keys, *earlier)


def mark_kernel(docs_hbm, mark_ref):
    mark_ref[...] = jnp.zeros_like(mark_ref)


def mark_of(doc_ids):
    return pl.pallas_call(
        mark_kernel,
        in_specs=[HBM],
        out_specs=VMEM,
        out_shape=pltpu.VMEM((8, HD), jnp.float32),
        name="mark",
        compiler_params=limit(1),
    )(doc_ids)


def copy_kernel(in_ref, out_ref):
    out_ref[...] = in_ref[...]


def held(x):
    return pl.pallas_call(
        copy_kernel,
        in_specs=[VMEM],
        out_specs=VMEM,
        out_shape=pltpu.VMEM(x.shape, x.dtype),
        name="held",
        compiler_params=limit(1),
        cost_estimate=AHEAD,
    )(x)


def in_hbm(x):
    return pltpu.with_memory_space_constraint(x, pltpu.HBM)


def per_device(queries, keys, values, grad_out, doc_ids):
    devices = lax.axis_size(AXES)
    ahead = [(i, i + (1 if i % 2 == 0 else 3)) for i in range(devices)]
    ahead = [pair for pair in ahead if pair[1] < devices]
    skip = [(i, i + 2) for i in range(devices - 2)]
    swap = [(i, i ^ 1) for i in range(devices)]
    back = [(b, a) for a, b in ahead]
    unskip = [(b, a) for a, b in skip]

    queries, grad_out = in_hbm(queries), in_hbm(grad_out)
    key_aside = lax.ppermute(keys, AXES, ahead)
    key_middle = lax.ppermute(keys, AXES, skip)
    qt, dot, queries, grad_out, bias, own_keys, size = stacked(doc_ids, queries, grad_out, in_hbm(keys))
    mark, late_values = lax.optimization_barrier(
        (mark_of(in_hbm(doc_ids.reshape(-1, ROWS))), values)
    )
    value_aside = lax.ppermute(late_values, AXES, ahead)
    value_middle = lax.ppermute(late_values, AXES, skip)
    key_paired = lax.ppermute(key_middle, AXES, swap)
    key_aside, key_middle, qt, grad_out, bias, own_keys, size = lax.optimization_barrier(
        (key_aside, key_middle, qt, grad_out, bias, own_keys, size)
    )
    key_blocks = [key_aside, key_middle, key_paired, own_keys]
    probs, dv_blocks = probs_and_dv(size, qt, held(bias), grad_out, key_blocks)
    dv_aside, dv_middle, dv_paired, dv_own = dv_blocks
    _, value_aside, value_middle = lax.optimization_barrier(
        (dv_paired, value_aside, value_middle)
    )
    value_paired = lax.ppermute(value_middle, AXES, swap)
    dv_other = lax.ppermute(dv_paired, AXES, swap)
    dv_far = lax.ppermute((dv_middle + dv_other).astype(jnp.bfloat16), AXES, unskip)
    dv_near = lax.ppermute(dv_aside, AXES, back)
    dscores, dk_blocks = dscores_and_dk(
        mark,
        queries,
        dot,
        probs,
        [value_aside, value_middle, value_paired, values],
    )
    dk_aside, dk_middle, dk_paired, dk_own = dk_blocks

    dk_other = lax.ppermute(dk_paired, AXES, swap)
    first_dq = dq_of(dscores, key_blocks, queries.shape, 0, 1)
    dk_other, first_dq = lax.optimization_barrier((dk_other, first_dq))
    dk_sum = (dk_middle + dk_other).astype(jnp.bfloat16)
    dk_far = lax.ppermute(dk_sum, AXES, unskip)
    dk_sum, dk_aside = lax.optimization_barrier((dk_sum, dk_aside))
    dk_near = lax.ppermute(dk_aside, AXES, back)
    grad_queries = dq_of(dscores, key_blocks, queries.shape, 1, KVH // GROUPS - 1, [first_dq])
    grad_keys = (dk_own + dk_near + dk_far).astype(jnp.bfloat16)
    grad_values = (dv_own + dv_near + dv_far).astype(jnp.bfloat16)
    return grad_queries, grad_keys, grad_values


def solution(mesh):
    split = P(AXES, None)
    return jax.shard_map(
        per_device,
        mesh=mesh,
        in_specs=(split, split, split, split, P()),
        out_specs=(split, split, split),
        check_vma=False,
    )
```

```python
import jax
import jax.numpy as jnp
from jax import lax
from jax.experimental import pallas as pl
from jax.experimental.pallas import tpu as pltpu
from jax.sharding import PartitionSpec as P

KVH = 8
HD = 128
G = 8
WINDOW = 384
ROWS = 128
SPAN = 4 * ROWS
STACK = G * ROWS
AXES = ("inner", "outer")
SCALE = 1.0 / HD**0.5
SCALE_LOG2 = 1.4426950408889634 / HD**0.5
HIDDEN = -1e30
KEY_MOST = 6.0
NT = (((1,), (1,)), ((), ()))
GROUPS = 2
PROBS_GROUPS = 4
MIB = 2**20
VMEM = pl.BlockSpec(memory_space=pltpu.VMEM)


def head_columns(group):
    return pl.ds(pl.multiple_of(group * HD, HD), HD)


def stacked_blocks(refs, group):
    return jnp.concatenate([ref[:, head_columns(group)] for ref in refs], axis=0)


def heads_of(ref, group):
    return [ref[:, head_columns(group * G + h)] for h in range(G)]


def put_blocks(refs, group, value):
    for i, ref in enumerate(refs):
        ref[:, head_columns(group)] = value[i * ROWS : (i + 1) * ROWS].astype(ref.dtype)


def put_bias(index, docs_ref, bias_ref):
    odd = lax.rem(index, 2)
    line = lax.broadcasted_iota(jnp.int32, (ROWS, ROWS), 0)
    lane = lax.broadcasted_iota(jnp.int32, (ROWS, ROWS), 1)

    def docs_of(block):
        row = docs_ref[pl.ds(jnp.maximum(block, 0), 1), :].astype(jnp.float32)
        return jnp.broadcast_to(row, (ROWS, ROWS))

    query_doc = docs_of(index)
    for i, offset in enumerate([3 - 2 * odd, 2, 1 + 2 * odd, 0]):
        gap = offset * ROWS + lane - line
        same = docs_of(index - offset).T == query_doc
        visible = (gap >= 0) & (gap < WINDOW) & (index >= offset) & same
        bias_ref[i * ROWS : (i + 1) * ROWS] = jnp.where(visible, 0.0, HIDDEN).astype(jnp.bfloat16)


def stack_kernel(docs_hbm, query_hbm, dout_hbm, keys_hbm, *refs):
    qt_ref, dot_ref, query_ref, dout_ref, bias_ref, own_ref, size_ref = refs[:7]
    docs_ref, sems, own_sem, docs_sem = refs[7:]
    loads = []
    for i, (source, target) in enumerate([(query_hbm, query_ref), (dout_hbm, dout_ref)]):
        for g in range(KVH):
            part = slice(g * STACK, (g + 1) * STACK)
            loads.append(
                pltpu.make_async_copy(source.at[:, part], target.at[:, part], sems.at[i, g])
            )
    own_load = pltpu.make_async_copy(keys_hbm, own_ref, own_sem)
    docs_load = pltpu.make_async_copy(docs_hbm, docs_ref, docs_sem)
    for load in [docs_load, *loads, own_load]:
        load.start()
    docs_load.wait()
    put_bias(lax.axis_index(AXES), docs_ref, bias_ref)
    size = jnp.zeros((1, STACK), jnp.float32)
    for g in range(KVH):
        loads[g].wait()
        loads[KVH + g].wait()
        for source, target in [(query_ref, qt_ref), (dout_ref, dot_ref)]:
            target[g] = jnp.concatenate([head.T for head in heads_of(source, g)], axis=1)
        sums = jnp.sum(jnp.abs(qt_ref[g].astype(jnp.float32)), axis=0, keepdims=True)
        size = jnp.maximum(size, sums)
    size_ref[...] = jnp.broadcast_to(size, size_ref.shape)
    own_load.wait()


def probs_kernel(size_ref, qt_ref, bias_ref, dout_ref, *refs):
    key_refs, probs_ref, dv_refs = refs[:4], refs[4], refs[5:9]
    bias = bias_ref[...]
    row = lax.broadcasted_iota(jnp.int32, (ROWS, STACK), 0)
    column = lax.broadcasted_iota(jnp.int32, (ROWS, STACK), 1)
    identity = jnp.where((column & (ROWS - 1)) == row, 1.0, 0.0).astype(jnp.bfloat16)

    def step(i, shift):
        groups = [i * PROBS_GROUPS + j for j in range(PROBS_GROUPS)]
        scores = [
            jnp.dot(
                jnp.concatenate([stacked_blocks(key_refs, g), bias], axis=1),
                jnp.concatenate([qt_ref[g], identity], axis=0),
                preferred_element_type=jnp.float32,
            )
            for g in groups
        ]
        for g, score in zip(groups, scores):
            if shift:
                score = score - jnp.max(score, axis=0, keepdims=True)
            powers = jnp.exp2(score * SCALE_LOG2)
            probs = powers * (1.0 / jnp.sum(powers, axis=0, keepdims=True))
            probs_b = probs.astype(jnp.bfloat16)
            probs_ref[g] = probs_b
            dout = jnp.concatenate(heads_of(dout_ref, g), axis=0)
            put_blocks(dv_refs, g, jnp.dot(probs_b, dout, preferred_element_type=jnp.float32))

    def run(shift):
        def body(i, carry):
            step(i, shift)
            return carry

        lax.fori_loop(0, KVH // PROBS_GROUPS, body, 0)

    small = jnp.max(size_ref[0:1]) * (KEY_MOST * SCALE_LOG2) <= 115.0
    pl.when(small)(lambda: run(False))
    pl.when(jnp.logical_not(small))(lambda: run(True))


def scores_kernel(mark_ref, query_ref, dot_ref, probs_ref, *refs):
    value_refs, dscores_ref, dk_refs = refs[:4], refs[4], refs[5:9]
    def step(i, carry):
        groups = [i * GROUPS + j for j in range(GROUPS)]
        deltas, dprobs = [], []
        for g in groups:
            values = stacked_blocks(value_refs, g)
            out = jnp.dot(values.T, probs_ref[g], preferred_element_type=jnp.float32)
            out = out.astype(jnp.bfloat16).astype(jnp.float32)
            deltas.append(jnp.sum(out * dot_ref[g].astype(jnp.float32), axis=0, keepdims=True))
            dprobs.append(jnp.dot(values, dot_ref[g], preferred_element_type=jnp.float32))
        for g, delta, dprob in zip(groups, deltas, dprobs):
            dscores = (probs_ref[g].astype(jnp.float32) * (dprob - delta)).astype(jnp.bfloat16)
            dscores_ref[g] = dscores
            query = jnp.concatenate(heads_of(query_ref, g), axis=0)
            dk = jnp.dot(dscores, query, preferred_element_type=jnp.float32)
            put_blocks(dk_refs, g, dk * SCALE)
        return carry

    lax.fori_loop(0, KVH // GROUPS, step, 0)


def queries_kernel(dscores_ref, *refs):
    key_refs, dq_ref = refs[:4], refs[-1]
    for g in range(GROUPS):
        keys = jnp.concatenate([ref[:, g * HD : (g + 1) * HD] for ref in key_refs], axis=0)
        dq = jnp.dot(keys.T, dscores_ref[g], preferred_element_type=jnp.float32) * SCALE
        for h in range(G):
            column = (g * G + h) * HD
            dq_ref[:, column : column + HD] = dq[:, h * HD : (h + 1) * HD].T.astype(dq_ref.dtype)


PAIRS = KVH * G * SPAN * ROWS


def cost(products, exponentials=0):
    return pl.CostEstimate(
        flops=PAIRS * HD * 2 * products, bytes_accessed=16 * MIB, transcendentals=exponentials
    )


AHEAD = pl.CostEstimate(flops=10**11, bytes_accessed=10**8, transcendentals=0)


def limit(mib):
    return pltpu.CompilerParams(vmem_limit_bytes=mib * MIB)


def bf16(*shape):
    return jax.ShapeDtypeStruct(shape, jnp.bfloat16)


def block_shapes():
    kinds = [jnp.bfloat16, jnp.float32, jnp.bfloat16, jnp.float32]
    return [jax.ShapeDtypeStruct((ROWS, KVH * HD), kind) for kind in kinds]


HBM = pl.BlockSpec(memory_space=pltpu.HBM)


def stacked(doc_ids, queries, grad_out, keys):
    flat = (KVH, HD, STACK)
    return pl.pallas_call(
        stack_kernel,
        in_specs=[HBM, HBM, HBM, HBM],
        out_specs=[VMEM] * 7,
        out_shape=[
            pltpu.VMEM(shape, jnp.bfloat16)
            for shape in (flat, flat, queries.shape, queries.shape, (SPAN, ROWS), keys.shape)
        ]
        + [pltpu.VMEM((8, STACK), jnp.float32)],
        scratch_shapes=[
            pltpu.VMEM((doc_ids.shape[0] // ROWS, ROWS), jnp.int32),
            pltpu.SemaphoreType.DMA((2, KVH)),
            pltpu.SemaphoreType.DMA,
            pltpu.SemaphoreType.DMA,
        ],
        name="stacked",
        compiler_params=limit(12),
    )(in_hbm(doc_ids.reshape(-1, ROWS)), queries, grad_out, keys)


def probs_and_dv(size, qt, bias, grad_out, keys):
    out = pl.pallas_call(
        probs_kernel,
        in_specs=[VMEM] * 8,
        out_specs=[VMEM] * 5,
        out_shape=[bf16(KVH, SPAN, STACK)] + block_shapes(),
        name="probs_and_dv",
        compiler_params=limit(16),
        cost_estimate=cost(2, PAIRS),
    )(size, qt, bias, grad_out, *keys)
    return out[0], out[1:]


def dscores_and_dk(mark, queries, dot, probs, values):
    out = pl.pallas_call(
        scores_kernel,
        in_specs=[VMEM] * 8,
        out_specs=[VMEM] * 5,
        out_shape=[bf16(KVH, SPAN, STACK)] + block_shapes(),
        input_output_aliases={3: 0},
        name="dscores_and_dk",
        compiler_params=limit(10),
        cost_estimate=cost(3),
    )(mark, queries, dot, probs, *values)
    return out[0], out[1:]


def dq_of(dscores, keys, shape):
    return pl.pallas_call(
        queries_kernel,
        grid=(KVH // GROUPS,),
        in_specs=[pl.BlockSpec((GROUPS, SPAN, STACK), lambda s: (s, 0, 0))]
        + [pl.BlockSpec((ROWS, GROUPS * HD), lambda s: (0, s))] * 4,
        out_specs=pl.BlockSpec((ROWS, GROUPS * G * HD), lambda s: (0, s)),
        out_shape=bf16(*shape),
        name="dq",
        compiler_params=limit(24),
        cost_estimate=cost(1),
    )(dscores, *keys)


def mark_kernel(docs_hbm, mark_ref):
    mark_ref[...] = jnp.zeros_like(mark_ref)


def mark_of(doc_ids):
    return pl.pallas_call(
        mark_kernel,
        in_specs=[HBM],
        out_specs=VMEM,
        out_shape=pltpu.VMEM((8, HD), jnp.float32),
        name="mark",
        compiler_params=limit(1),
    )(doc_ids)


def copy_kernel(in_ref, out_ref):
    out_ref[...] = in_ref[...]


def held(x):
    return pl.pallas_call(
        copy_kernel,
        in_specs=[VMEM],
        out_specs=VMEM,
        out_shape=pltpu.VMEM(x.shape, x.dtype),
        name="held",
        compiler_params=limit(2),
        cost_estimate=AHEAD,
    )(x)


def in_hbm(x):
    return pltpu.with_memory_space_constraint(x, pltpu.HBM)


def per_device(queries, keys, values, grad_out, doc_ids):
    devices = lax.axis_size(AXES)
    ahead = [(i, i + (1 if i % 2 == 0 else 3)) for i in range(devices)]
    ahead = [pair for pair in ahead if pair[1] < devices]
    skip = [(i, i + 2) for i in range(devices - 2)]
    swap = [(i, i ^ 1) for i in range(devices)]
    back = [(b, a) for a, b in ahead]
    unskip = [(b, a) for a, b in skip]

    queries, grad_out = in_hbm(queries), in_hbm(grad_out)
    key_aside = lax.ppermute(keys, AXES, ahead)
    key_middle = lax.ppermute(keys, AXES, skip)
    qt, dot, queries, grad_out, bias, own_keys, size = stacked(doc_ids, queries, grad_out, in_hbm(keys))
    mark, late_values = lax.optimization_barrier(
        (mark_of(in_hbm(doc_ids.reshape(-1, ROWS))), values)
    )
    value_aside = lax.ppermute(late_values, AXES, ahead)
    value_middle = lax.ppermute(late_values, AXES, skip)
    key_paired = lax.ppermute(key_middle, AXES, swap)
    key_aside, key_middle, qt, grad_out, bias, own_keys, size = lax.optimization_barrier(
        (key_aside, key_middle, qt, grad_out, bias, own_keys, size)
    )
    key_blocks = [key_aside, key_middle, key_paired, own_keys]
    probs, dv_blocks = probs_and_dv(size, qt, held(bias), grad_out, key_blocks)
    dv_aside, dv_middle, dv_paired, dv_own = dv_blocks
    _, value_aside, value_middle = lax.optimization_barrier(
        (dv_paired, value_aside, value_middle)
    )
    value_paired = lax.ppermute(value_middle, AXES, swap)
    dv_other = lax.ppermute(dv_paired, AXES, swap)
    dv_far = lax.ppermute((dv_middle + dv_other).astype(jnp.bfloat16), AXES, unskip)
    dv_near = lax.ppermute(dv_aside, AXES, back)
    dscores, dk_blocks = dscores_and_dk(
        mark,
        queries,
        dot,
        probs,
        [value_aside, value_middle, value_paired, values],
    )
    dk_aside, dk_middle, dk_paired, dk_own = dk_blocks

    dk_other = lax.ppermute(dk_paired, AXES, swap)
    dk_other, dk_own = lax.optimization_barrier((dk_other, held(dk_own)))
    dk_sum = (dk_middle + dk_other).astype(jnp.bfloat16)
    dk_far = lax.ppermute(dk_sum, AXES, unskip)
    dk_sum, dk_aside = lax.optimization_barrier((dk_sum, dk_aside))
    dk_near = lax.ppermute(dk_aside, AXES, back)
    grad_queries = dq_of(dscores, key_blocks, queries.shape)
    grad_keys = (dk_own + dk_near + dk_far).astype(jnp.bfloat16)
    grad_values = (dv_own + dv_near + dv_far).astype(jnp.bfloat16)
    return grad_queries, grad_keys, grad_values


def solution(mesh):
    split = P(AXES, None)
    return jax.shard_map(
        per_device,
        mesh=mesh,
        in_specs=(split, split, split, split, P()),
        out_specs=(split, split, split),
        check_vma=False,
    )
```

```python
import jax
import jax.numpy as jnp
from jax import lax
from jax.experimental import pallas as pl
from jax.experimental.pallas import tpu as pltpu
from jax.sharding import PartitionSpec as P

KVH = 8
HD = 128
G = 8
WINDOW = 384
ROWS = 128
SPAN = 4 * ROWS
STACK = G * ROWS
AXES = ("inner", "outer")
SCALE = 1.0 / HD**0.5
SCALE_LOG2 = 1.4426950408889634 / HD**0.5
HIDDEN = -1e30
KEY_MOST = 6.0
NT = (((1,), (1,)), ((), ()))
GROUPS = 2
PROBS_GROUPS = 4
MIB = 2**20
VMEM = pl.BlockSpec(memory_space=pltpu.VMEM)


def head_columns(group):
    return pl.ds(pl.multiple_of(group * HD, HD), HD)


def stacked_blocks(refs, group):
    return jnp.concatenate([ref[:, head_columns(group)] for ref in refs], axis=0)


def heads_of(ref, group):
    return [ref[:, head_columns(group * G + h)] for h in range(G)]


def put_blocks(refs, group, value):
    for i, ref in enumerate(refs):
        ref[:, head_columns(group)] = value[i * ROWS : (i + 1) * ROWS].astype(ref.dtype)


def put_bias(index, docs_ref, bias_ref):
    odd = lax.rem(index, 2)
    line = lax.broadcasted_iota(jnp.int32, (ROWS, ROWS), 0)
    lane = lax.broadcasted_iota(jnp.int32, (ROWS, ROWS), 1)

    def docs_of(block):
        row = docs_ref[pl.ds(jnp.maximum(block, 0), 1), :].astype(jnp.float32)
        return jnp.broadcast_to(row, (ROWS, ROWS))

    query_doc = docs_of(index)
    for i, offset in enumerate([3 - 2 * odd, 2, 1 + 2 * odd, 0]):
        gap = offset * ROWS + lane - line
        same = docs_of(index - offset).T == query_doc
        visible = (gap >= 0) & (gap < WINDOW) & (index >= offset) & same
        bias_ref[i * ROWS : (i + 1) * ROWS] = jnp.where(visible, 0.0, HIDDEN).astype(jnp.bfloat16)


def stack_kernel(docs_hbm, query_hbm, dout_hbm, keys_hbm, *refs):
    qt_ref, dot_ref, query_ref, dout_ref, bias_ref, own_ref, size_ref = refs[:7]
    docs_ref, sems, own_sem, docs_sem = refs[7:]
    loads = []
    for i, (source, target) in enumerate([(query_hbm, query_ref), (dout_hbm, dout_ref)]):
        for g in range(KVH):
            part = slice(g * STACK, (g + 1) * STACK)
            loads.append(
                pltpu.make_async_copy(source.at[:, part], target.at[:, part], sems.at[i, g])
            )
    own_load = pltpu.make_async_copy(keys_hbm, own_ref, own_sem)
    docs_load = pltpu.make_async_copy(docs_hbm, docs_ref, docs_sem)
    for load in [docs_load, *loads, own_load]:
        load.start()
    docs_load.wait()
    put_bias(lax.axis_index(AXES), docs_ref, bias_ref)
    size = jnp.zeros((1, STACK), jnp.float32)
    for g in range(KVH):
        loads[g].wait()
        loads[KVH + g].wait()
        for source, target in [(query_ref, qt_ref), (dout_ref, dot_ref)]:
            target[g] = jnp.concatenate([head.T for head in heads_of(source, g)], axis=1)
        sums = jnp.sum(jnp.abs(qt_ref[g].astype(jnp.float32)), axis=0, keepdims=True)
        size = jnp.maximum(size, sums)
    size_ref[...] = jnp.broadcast_to(size, size_ref.shape)
    own_load.wait()


def probs_kernel(size_ref, qt_ref, bias_ref, dout_ref, *refs):
    key_refs, probs_ref, dv_refs = refs[:4], refs[4], refs[5:9]
    bias = bias_ref[...]
    row = lax.broadcasted_iota(jnp.int32, (ROWS, STACK), 0)
    column = lax.broadcasted_iota(jnp.int32, (ROWS, STACK), 1)
    identity = jnp.where((column & (ROWS - 1)) == row, 1.0, 0.0).astype(jnp.bfloat16)

    def step(i, shift):
        groups = [i * PROBS_GROUPS + j for j in range(PROBS_GROUPS)]
        scores = [
            jnp.dot(
                jnp.concatenate([stacked_blocks(key_refs, g), bias], axis=1),
                jnp.concatenate([qt_ref[g], identity], axis=0),
                preferred_element_type=jnp.float32,
            )
            for g in groups
        ]
        for g, score in zip(groups, scores):
            if shift:
                score = score - jnp.max(score, axis=0, keepdims=True)
            powers = jnp.exp2(score * SCALE_LOG2)
            probs = powers * (1.0 / jnp.sum(powers, axis=0, keepdims=True))
            probs_b = probs.astype(jnp.bfloat16)
            probs_ref[g] = probs_b
            dout = jnp.concatenate(heads_of(dout_ref, g), axis=0)
            put_blocks(dv_refs, g, jnp.dot(probs_b, dout, preferred_element_type=jnp.float32))

    def run(shift):
        def body(i, carry):
            step(i, shift)
            return carry

        lax.fori_loop(0, KVH // PROBS_GROUPS, body, 0)

    small = jnp.max(size_ref[0:1]) * (KEY_MOST * SCALE_LOG2) <= 115.0
    pl.when(small)(lambda: run(False))
    pl.when(jnp.logical_not(small))(lambda: run(True))


def scores_kernel(mark_ref, query_ref, dot_ref, probs_ref, *refs):
    value_refs, dscores_ref, dk_refs = refs[:4], refs[4], refs[5:9]
    def step(i, carry):
        groups = [i * GROUPS + j for j in range(GROUPS)]
        deltas, dprobs = [], []
        for g in groups:
            values = stacked_blocks(value_refs, g)
            out = jnp.dot(values.T, probs_ref[g], preferred_element_type=jnp.float32)
            out = out.astype(jnp.bfloat16).astype(jnp.float32)
            deltas.append(jnp.sum(out * dot_ref[g].astype(jnp.float32), axis=0, keepdims=True))
        for g in groups:
            values = stacked_blocks(value_refs, g)
            dprobs.append(jnp.dot(values, dot_ref[g], preferred_element_type=jnp.float32))
        for g, delta, dprob in zip(groups, deltas, dprobs):
            dscores = (probs_ref[g].astype(jnp.float32) * (dprob - delta)).astype(jnp.bfloat16)
            dscores_ref[g] = dscores
            query = jnp.concatenate(heads_of(query_ref, g), axis=0)
            dk = jnp.dot(dscores, query, preferred_element_type=jnp.float32)
            put_blocks(dk_refs, g, dk * SCALE)
        return carry

    lax.fori_loop(0, KVH // GROUPS, step, 0)


def queries_kernel(dscores_ref, *refs):
    key_refs, dq_ref = refs[:4], refs[-1]
    for g in range(GROUPS):
        keys = jnp.concatenate([ref[:, g * HD : (g + 1) * HD] for ref in key_refs], axis=0)
        dq = jnp.dot(keys.T, dscores_ref[g], preferred_element_type=jnp.float32) * SCALE
        for h in range(G):
            column = (g * G + h) * HD
            dq_ref[:, column : column + HD] = dq[:, h * HD : (h + 1) * HD].T.astype(dq_ref.dtype)


PAIRS = KVH * G * SPAN * ROWS


def cost(products, exponentials=0):
    return pl.CostEstimate(
        flops=PAIRS * HD * 2 * products, bytes_accessed=16 * MIB, transcendentals=exponentials
    )


AHEAD = pl.CostEstimate(flops=10**11, bytes_accessed=10**8, transcendentals=0)


def limit(mib):
    return pltpu.CompilerParams(vmem_limit_bytes=mib * MIB)


def bf16(*shape):
    return jax.ShapeDtypeStruct(shape, jnp.bfloat16)


def block_shapes():
    kinds = [jnp.bfloat16, jnp.float32, jnp.bfloat16, jnp.float32]
    return [jax.ShapeDtypeStruct((ROWS, KVH * HD), kind) for kind in kinds]


HBM = pl.BlockSpec(memory_space=pltpu.HBM)


def stacked(doc_ids, queries, grad_out, keys):
    flat = (KVH, HD, STACK)
    return pl.pallas_call(
        stack_kernel,
        in_specs=[HBM, HBM, HBM, HBM],
        out_specs=[VMEM] * 7,
        out_shape=[
            pltpu.VMEM(shape, jnp.bfloat16)
            for shape in (flat, flat, queries.shape, queries.shape, (SPAN, ROWS), keys.shape)
        ]
        + [pltpu.VMEM((8, STACK), jnp.float32)],
        scratch_shapes=[
            pltpu.VMEM((doc_ids.shape[0] // ROWS, ROWS), jnp.int32),
            pltpu.SemaphoreType.DMA((2, KVH)),
            pltpu.SemaphoreType.DMA,
            pltpu.SemaphoreType.DMA,
        ],
        name="stacked",
        compiler_params=limit(12),
    )(in_hbm(doc_ids.reshape(-1, ROWS)), queries, grad_out, keys)


def probs_and_dv(size, qt, bias, grad_out, keys):
    out = pl.pallas_call(
        probs_kernel,
        in_specs=[VMEM] * 8,
        out_specs=[VMEM] * 5,
        out_shape=[bf16(KVH, SPAN, STACK)] + block_shapes(),
        name="probs_and_dv",
        compiler_params=limit(16),
        cost_estimate=cost(2, PAIRS),
    )(size, qt, bias, grad_out, *keys)
    return out[0], out[1:]


def dscores_and_dk(mark, queries, dot, probs, values):
    out = pl.pallas_call(
        scores_kernel,
        in_specs=[VMEM] * 8,
        out_specs=[VMEM] * 5,
        out_shape=[bf16(KVH, SPAN, STACK)] + block_shapes(),
        input_output_aliases={3: 0},
        name="dscores_and_dk",
        compiler_params=limit(10),
        cost_estimate=cost(3),
    )(mark, queries, dot, probs, *values)
    return out[0], out[1:]


def dq_of(dscores, keys, shape):
    return pl.pallas_call(
        queries_kernel,
        grid=(KVH // GROUPS,),
        in_specs=[pl.BlockSpec((GROUPS, SPAN, STACK), lambda s: (s, 0, 0))]
        + [pl.BlockSpec((ROWS, GROUPS * HD), lambda s: (0, s))] * 4,
        out_specs=pl.BlockSpec((ROWS, GROUPS * G * HD), lambda s: (0, s)),
        out_shape=bf16(*shape),
        name="dq",
        compiler_params=limit(24),
        cost_estimate=cost(1),
    )(dscores, *keys)


def mark_kernel(docs_hbm, mark_ref):
    mark_ref[...] = jnp.zeros_like(mark_ref)


def mark_of(doc_ids):
    return pl.pallas_call(
        mark_kernel,
        in_specs=[HBM],
        out_specs=VMEM,
        out_shape=pltpu.VMEM((8, HD), jnp.float32),
        name="mark",
        compiler_params=limit(1),
    )(doc_ids)


def copy_kernel(in_ref, out_ref):
    out_ref[...] = in_ref[...]


def held(x):
    return pl.pallas_call(
        copy_kernel,
        in_specs=[VMEM],
        out_specs=VMEM,
        out_shape=pltpu.VMEM(x.shape, x.dtype),
        name="held",
        compiler_params=limit(2),
        cost_estimate=AHEAD,
    )(x)


def in_hbm(x):
    return pltpu.with_memory_space_constraint(x, pltpu.HBM)


def per_device(queries, keys, values, grad_out, doc_ids):
    devices = lax.axis_size(AXES)
    ahead = [(i, i + (1 if i % 2 == 0 else 3)) for i in range(devices)]
    ahead = [pair for pair in ahead if pair[1] < devices]
    skip = [(i, i + 2) for i in range(devices - 2)]
    swap = [(i, i ^ 1) for i in range(devices)]
    back = [(b, a) for a, b in ahead]
    unskip = [(b, a) for a, b in skip]

    queries, grad_out = in_hbm(queries), in_hbm(grad_out)
    key_aside = lax.ppermute(keys, AXES, ahead)
    key_middle = lax.ppermute(keys, AXES, skip)
    qt, dot, queries, grad_out, bias, own_keys, size = stacked(doc_ids, queries, grad_out, in_hbm(keys))
    mark, late_values = lax.optimization_barrier(
        (mark_of(in_hbm(doc_ids.reshape(-1, ROWS))), values)
    )
    value_aside = lax.ppermute(late_values, AXES, ahead)
    value_middle = lax.ppermute(late_values, AXES, skip)
    key_paired = lax.ppermute(key_middle, AXES, swap)
    key_aside, key_middle, qt, grad_out, bias, own_keys, size = lax.optimization_barrier(
        (key_aside, key_middle, qt, grad_out, bias, own_keys, size)
    )
    key_blocks = [key_aside, key_middle, key_paired, own_keys]
    probs, dv_blocks = probs_and_dv(size, qt, held(bias), grad_out, key_blocks)
    dv_aside, dv_middle, dv_paired, dv_own = dv_blocks
    _, value_aside, value_middle = lax.optimization_barrier(
        (dv_paired, value_aside, value_middle)
    )
    value_paired = lax.ppermute(value_middle, AXES, swap)
    dv_other = lax.ppermute(dv_paired, AXES, swap)
    dv_far = lax.ppermute((dv_middle + dv_other).astype(jnp.bfloat16), AXES, unskip)
    dv_near = lax.ppermute(dv_aside, AXES, back)
    dscores, dk_blocks = dscores_and_dk(
        mark,
        queries,
        dot,
        probs,
        [value_aside, value_middle, value_paired, values],
    )
    dk_aside, dk_middle, dk_paired, dk_own = dk_blocks

    dk_other = lax.ppermute(dk_paired, AXES, swap)
    dk_other, dk_own = lax.optimization_barrier((dk_other, held(dk_own)))
    dk_sum = (dk_middle + dk_other).astype(jnp.bfloat16)
    dk_far = lax.ppermute(dk_sum, AXES, unskip)
    dk_sum, dk_aside = lax.optimization_barrier((dk_sum, dk_aside))
    dk_near = lax.ppermute(dk_aside, AXES, back)
    grad_queries = dq_of(dscores, key_blocks, queries.shape)
    grad_keys = (dk_own + dk_near + dk_far).astype(jnp.bfloat16)
    grad_values = (dv_own + dv_near + dv_far).astype(jnp.bfloat16)
    return grad_queries, grad_keys, grad_values


def solution(mesh):
    split = P(AXES, None)
    return jax.shard_map(
        per_device,
        mesh=mesh,
        in_specs=(split, split, split, split, P()),
        out_specs=(split, split, split),
        check_vma=False,
    )
```
